32 devices in a mesh: row: 4 (over x, core), col: 8 (over z, y).
Axes of the slice: x: 2, y: 2, z: 4, core: 2. Of those that a mesh axis runs over, the one named last changes fastest.
Arguments:
- amplitudes: float32 [2048, 256], P('row', 'col'), may hold values from -6 to 6
- integrals: float32 [256, 2048], P('row', 'col'), may hold values from -0.375 to 0.375
- occ_counts: int32 [8], replicated, may hold values from 1 to 10, 40 in all
- vir_counts: int32 [8], replicated, may hold values from 1 to 80, 400 in all
Outputs:
- symmetrized: float32 [2048, 2048], P('row', 'col')
The draws below stay inside these ranges and needn't reach their ends.
Inputs may be any that keep to these rules, and one draw needn't show every extreme that they name: `occ_counts`: counts of occupied orbitals in the 8 irreducible representations, summing to 40. `vir_counts`: counts of virtual orbitals in the 8 irreducible representations, summing to 400.
All inputs are finite; a program needn't handle non-finite values.
Results may differ from the reference program's by a relative error of at most 0.00007.
Values sent between devices are 32-bit elements; how exact they have to be, the bound alone decides.
No kernel may reach another device: no remote copies, remote signals or barrier semaphores. Data moves between devices by JAX's collectives and lax.ppermute only.
A program may use at most 64 MiB of HBM per device.

```python
import math
import jax
import jax.numpy as jnp
import numpy as np
from jax import lax

NOCC = 40
NVIR = 400
IRREPS = 8
KW = 256
PAIRS = 2048


def block_scale(rng, extent, pieces, smallest, top_value):
    factor_of = 1.0
    for position, parts in pieces:
        draws = jax.random.uniform(jax.random.fold_in(jax.random.fold_in(rng, 6), position), (parts,), jnp.float32, smallest / len(pieces), top_value / len(pieces))
        factor_of = factor_of * jnp.repeat(jnp.exp(draws), extent[position] // parts).reshape((-1,) + (1,) * (len(extent) - 1 - position))
    return factor_of


def split_up(number_of, total, reach, lean):
    weights = [(1 << 20) // math.isqrt(grade ** lean) + 1 for grade in range(2, number_of + 1)]
    rest, given = total - reach - (number_of - 1), [1] * (number_of - 1)
    while rest > 0:
        movable = [i for i in range(number_of - 1) if given[i] < reach]
        whole, left = sum([weights[i] for i in movable]), rest
        for i in movable:
            extra = min(reach - given[i], max(1, left * weights[i] // whole), rest)
            given[i] = given[i] + extra
            rest = rest - extra
    return np.array([reach] + given)


def ragged_sizes(own_key, amount, total, bound, lean):
    if amount == 2:
        one = jax.random.randint(own_key, (), max(1, total - bound), min(bound, total - 1) + 1)
        return jnp.stack([one, total - one])
    sizes = jnp.asarray(split_up(amount, total, bound, lean), jnp.int32)
    pairs = (amount - 1) // 2
    source_of, sink = sizes[1:1 + 2 * pairs:2], sizes[2:2 + 2 * pairs:2]
    room = jnp.minimum(source_of - 1, bound - sink)
    shifted = jax.random.randint(jax.random.fold_in(own_key, 1), (pairs,), 0, 1 << 20) % (room + 1)
    sizes = sizes.at[1:1 + 2 * pairs:2].set(source_of - shifted).at[2:2 + 2 * pairs:2].set(sink + shifted)
    return sizes[jax.random.permutation(jax.random.fold_in(own_key, 2), amount)]


def bell_draw(rng, dims, width, most, pieces=(), held_as=jnp.bfloat16):
    gain = block_scale(rng, dims, pieces, -0.22, 0.18) if pieces else 1.0
    array = jax.random.normal(rng, dims, jnp.float32) * width * gain
    return jnp.minimum(jnp.maximum(array, -most), most).astype(held_as)


def setup_inputs(seed: int = 0) -> dict:
    arg_keys = jax.random.split(jax.random.key(seed), 5)
    amplitudes = bell_draw(arg_keys[0], (PAIRS, KW), 1.0, 6.0, ((0, 4), (1, 8)), jnp.float32)
    integrals = bell_draw(arg_keys[1], (KW, PAIRS), KW ** -0.5, 0.375, ((0, 4), (1, 8)), jnp.float32)
    occ_counts = ragged_sizes(arg_keys[2], IRREPS, NOCC, NOCC // 4, 1).astype(jnp.int32)
    vir_counts = ragged_sizes(arg_keys[3], IRREPS, NVIR, NVIR // 5, 1).astype(jnp.int32)
    return {"amplitudes": amplitudes, "integrals": integrals, "occ_counts": occ_counts, "vir_counts": vir_counts}


def orbital_irreps(orbitals, counts):
    bounds = jnp.cumsum(counts)[:-1]
    return jnp.sum((orbitals[:, None] >= bounds[None, :]).astype(jnp.int32), axis=1)


def pair_labels(positions, occ_counts, vir_counts):
    occ_part = orbital_irreps(positions // NVIR, occ_counts)
    vir_part = orbital_irreps(positions % NVIR, vir_counts)
    return jnp.bitwise_xor(occ_part, vir_part)


def reference(amplitudes, integrals, occ_counts, vir_counts):
    cycle = jnp.dot(amplitudes, integrals, precision=lax.Precision.HIGHEST, preferred_element_type=jnp.float32)
    labels = pair_labels(jnp.arange(PAIRS, dtype=jnp.int32), occ_counts, vir_counts)
    allowed = labels[:, None] == labels[None, :]
    return jnp.where(allowed, cycle + cycle.T, 0.0)
```

```python
import functools
import jax
import jax.numpy as jnp
from jax import lax
from jax.experimental import pallas as pl
from jax.experimental.pallas import tpu as pltpu
from jax.sharding import PartitionSpec as P

NVIR = 400
IRREPS = 8


def labels_of(pos, occ, vir):
    occ_of = pos // NVIR
    vir_of = pos - occ_of * NVIR
    one = jnp.zeros_like(pos)
    two = jnp.zeros_like(pos)
    for bound in occ:
        one = one + jnp.where(occ_of >= bound, 1, 0)
    for bound in vir:
        two = two + jnp.where(vir_of >= bound, 1, 0)
    return one ^ two


def finish(sizes, *refs):
    nr, nc, tall, narrow, ka, kb = sizes
    nz, nx = nc // 2, nr // 2
    occ_ref, vir_ref = refs[:2]
    a_refs = refs[2 : 2 + nc]
    refs = refs[2 + nc :]
    bm_refs, refs = refs[:nc], refs[nc:]
    b_refs, refs = refs[:nr], refs[nr:]
    ac_refs, refs = refs[:2], refs[2:]
    out_ref, left, right = refs
    row, col = lax.axis_index("row"), lax.axis_index("col")
    z, y = col // 2, lax.rem(col, 2)
    kw = ka * nc
    for d in range(nc):
        at = pl.multiple_of((col ^ d) * ka, ka)
        left[pl.ds(at, ka), :] = a_refs[d][...]
        at = pl.multiple_of(kw + (z ^ (d // 2)) * kb, kb)
        lane = pl.multiple_of((y ^ (d % 2)) * narrow, narrow)
        left[pl.ds(at, kb), pl.ds(lane, narrow)] = bm_refs[d][...]
    for d in range(nr):
        at = pl.multiple_of((row ^ d) * kb, kb)
        right[pl.ds(at, kb), :] = b_refs[d][...]
    for d in range(nc):
        at = pl.multiple_of(kw + (col ^ d) * ka, ka)
        rows = pl.ds(d * ka, ka)
        right[pl.ds(at, ka), :] = ac_refs[0][rows, :] + ac_refs[1][rows, :]
    lw = left[...]
    rw = right[...]
    lh = lw.astype(jnp.bfloat16)
    ll = (lw - lh.astype(jnp.float32)).astype(jnp.bfloat16)
    rh = rw.astype(jnp.bfloat16)
    rl = (rw - rh.astype(jnp.float32)).astype(jnp.bfloat16)

    def mm(one, two):
        return lax.dot_general(one, two, (((0,), (0,)), ((), ())), preferred_element_type=jnp.float32)

    total = mm(lh, rl) + mm(ll, rh) + mm(lh, rh)
    occ, vir = [], []
    one = two = 0
    for h in range(IRREPS - 1):
        one, two = one + occ_ref[h], two + vir_ref[h]
        occ.append(one)
        vir.append(two)
    rl_ = labels_of(row * tall + lax.broadcasted_iota(jnp.int32, (tall, 1), 0), occ, vir)
    cl_ = labels_of(col * narrow + lax.broadcasted_iota(jnp.int32, (1, narrow), 1), occ, vir)
    out_ref[...] = jnp.where(rl_ == cl_, total, 0.0)


def per_device(sizes, amplitudes, integrals, occ_counts, vir_counts):
    nr, nc, tall, narrow, ka, kb = sizes
    nz, nx = nc // 2, nr // 2
    row, col = lax.axis_index("row"), lax.axis_index("col")
    z, y = col // 2, lax.rem(col, 2)

    def send(value, pairs):
        return lax.ppermute(value, ("row", "col"), pairs)

    def moved(dr, dc, keep=lambda r, c: True):
        return [(r * nc + c, (r ^ dr) * nc + (c ^ dc)) for r in range(nr) for c in range(nc) if keep(r, c)]

    mirror = [(zz * nc + 2 * r + h, r * nc + 2 * zz + h) for r in range(nr) for zz in range(nz) for h in range(2)]
    at = amplitudes.T
    a = [None] * nc
    a[0] = at
    for d in range(nz - 1, 0, -1):
        a[2 * d] = send(at, moved(0, 2 * d))
    bm = send(integrals, mirror)
    b = [None] * nr
    b[0] = integrals
    for d in range(2, nr, 2):
        b[d] = send(integrals, moved(d, 0))
    for d in range(0, nr, 2):
        b[d + 1] = send(b[d], moved(1, 0))
    m = [None] * nc
    m[0] = bm
    for d in range(nz - 1, 0, -1):
        m[2 * d] = send(bm, moved(0, 2 * d))
    ay = send(jnp.concatenate(a[0::2], 0), moved(0, 1))
    for d in range(nz):
        a[2 * d + 1] = ay[d * ka : (d + 1) * ka]
    my = send(jnp.concatenate(m[0::2], 0), moved(0, 1))
    for d in range(nz):
        m[2 * d + 1] = my[d * kb : (d + 1) * kb]
    own = jnp.concatenate([lax.dynamic_slice_in_dim(v, y * narrow, narrow, 1) for v in a], axis=0)
    own = jnp.where(row == z, own, 0.0)
    own = lax.optimization_barrier((own, *m[2::2], *b))[0]
    acx = own
    for d in range(2, nr, 2):
        acx = acx + send(own, moved(d, 0, lambda r, c: r == c // 2))
    acx = lax.optimization_barrier((acx, *m[1::2]))[0]
    ack = send(acx, moved(1, 0, lambda r, c: r % 2 == (c // 2) % 2))
    smem = pl.BlockSpec(memory_space=pltpu.SMEM)
    vmem = pl.BlockSpec(memory_space=pltpu.VMEM)
    return pl.pallas_call(
        functools.partial(finish, sizes),
        out_shape=jax.ShapeDtypeStruct((tall, narrow), jnp.float32),
        in_specs=[smem, smem] + [vmem] * (2 * nc + nr + 2),
        out_specs=vmem,
        scratch_shapes=[
            pltpu.VMEM((ka * nc + kb * nr, tall), jnp.float32),
            pltpu.VMEM((ka * nc + kb * nr, narrow), jnp.float32),
        ],
        compiler_params=pltpu.CompilerParams(vmem_limit_bytes=40 * 1024 * 1024),
    )(occ_counts, vir_counts, *a, *m, *b, acx, ack)


def solution(mesh):
    nr, nc = mesh.shape["row"], mesh.shape["col"]

    def whole(amplitudes, integrals, occ_counts, vir_counts):
        pairs, kw = amplitudes.shape
        sizes = (nr, nc, pairs // nr, pairs // nc, kw // nc, kw // nr)
        placed = (P("row", "col"), P("row", "col"), P(), P())
        return jax.shard_map(
            functools.partial(per_device, sizes), mesh=mesh, in_specs=placed, out_specs=P("row", "col"), check_vma=False
        )(amplitudes, integrals, occ_counts, vir_counts)

    return whole
```

```python
import functools
import jax
import jax.numpy as jnp
from jax import lax
from jax.experimental import pallas as pl
from jax.experimental.pallas import tpu as pltpu
from jax.sharding import PartitionSpec as P

NVIR = 400
IRREPS = 8


def labels_of(pos, occ, vir):
    occ_of = pos // NVIR
    vir_of = pos - occ_of * NVIR
    one = jnp.zeros_like(pos)
    two = jnp.zeros_like(pos)
    for bound in occ:
        one = one + jnp.where(occ_of >= bound, 1, 0)
    for bound in vir:
        two = two + jnp.where(vir_of >= bound, 1, 0)
    return one ^ two


def halves(value):
    high = value.astype(jnp.bfloat16)
    return high, (value - high.astype(jnp.float32)).astype(jnp.bfloat16)


def product(left, right):
    def mm(one, two):
        return lax.dot_general(one, two, (((0,), (0,)), ((), ())), preferred_element_type=jnp.float32)

    (lh, ll), (rh, rl) = halves(left), halves(right)
    return mm(lh, rl) + mm(ll, rh) + mm(lh, rh)


def direct(sizes, *refs):
    nr, nc, tall, narrow, ka, kb = sizes
    occ_ref, vir_ref = refs[:2]
    a_refs, b_refs = refs[2 : 2 + nc], refs[2 + nc : 2 + nc + nr]
    out_ref, mask_ref, left, right = refs[2 + nc + nr :]
    row, col = lax.axis_index("row"), lax.axis_index("col")
    for d in range(nc):
        left[pl.ds(pl.multiple_of((col ^ d) * ka, ka), ka), :] = a_refs[d][...]
    for d in range(nr):
        right[pl.ds(pl.multiple_of((row ^ d) * kb, kb), kb), :] = b_refs[d][...]
    out_ref[...] = product(left[...], right[...])
    occ, vir = [], []
    one = two = 0
    for h in range(IRREPS - 1):
        one, two = one + occ_ref[h], two + vir_ref[h]
        occ.append(one)
        vir.append(two)
    rows = labels_of(row * tall + lax.broadcasted_iota(jnp.int32, (tall, 1), 0), occ, vir)
    cols = labels_of(col * narrow + lax.broadcasted_iota(jnp.int32, (1, narrow), 1), occ, vir)
    mask_ref[...] = jnp.where(rows == cols, 1.0, 0.0)


def mirrored(sizes, *refs):
    nr, nc, tall, narrow, ka, kb = sizes
    nz = nc // 2
    part_ref, mask_ref = refs[:2]
    m_refs, ac_refs = refs[2 : 2 + nc], refs[2 + nc : 4 + nc]
    out_ref, left, right = refs[4 + nc :]
    col = lax.axis_index("col")
    z, y = col // 2, lax.rem(col, 2)
    for d in range(nc):
        at = pl.multiple_of((z ^ (d // 2)) * kb, kb)
        lane = pl.multiple_of((y ^ (d % 2)) * narrow, narrow)
        left[pl.ds(at, kb), pl.ds(lane, narrow)] = m_refs[d][...]
        at = pl.multiple_of((col ^ d) * ka, ka)
        rows = pl.ds((d % 2 * nz + d // 2) * ka, ka)
        right[pl.ds(at, ka), :] = ac_refs[0][rows, :] + ac_refs[1][rows, :]
    total = part_ref[...] + product(left[...], right[...])
    out_ref[...] = jnp.where(mask_ref[...] > 0.0, total, 0.0)


def per_device(sizes, amplitudes, integrals, occ_counts, vir_counts):
    nr, nc, tall, narrow, ka, kb = sizes
    nz = nc // 2
    row, col = lax.axis_index("row"), lax.axis_index("col")
    z, y = col // 2, lax.rem(col, 2)

    def send(value, pairs):
        return lax.ppermute(value, ("row", "col"), pairs)

    def moved(dr, dc, keep=lambda r, c: True):
        return [(r * nc + c, (r ^ dr) * nc + (c ^ dc)) for r in range(nr) for c in range(nc) if keep(r, c)]

    def mirror(e):
        return [(r * nc + c, (c // 2) * nc + 2 * (r ^ e) + c % 2) for r in range(nr) for c in range(nc)]

    def after(value, *others):
        return lax.optimization_barrier((value, *others))[0]

    def half_of(chunks, part):
        return jnp.concatenate([lax.dynamic_slice_in_dim(v, part * narrow, narrow, 1) for v in chunks], axis=0)

    def home(r, c):
        return r == c // 2

    def core(r, c):
        return r % 2 == (c // 2) % 2

    at = amplitudes.T
    a = [None] * nc
    a[0] = at
    m = [None] * nc
    b = [None] * nr
    b[0] = integrals
    for d in range(nz - 1, 0, -1):
        a[2 * d] = send(at, moved(0, 2 * d))
    for e in range(0, nz, 2):
        m[2 * e] = send(integrals, mirror(e))
    for d in range(2, nr, 2):
        b[d] = send(after(integrals, *a[2::2]), moved(d, 0))
    ay = send(jnp.concatenate(a[0::2], 0), moved(0, 1))
    for d in range(nz):
        a[2 * d + 1] = ay[d * ka : (d + 1) * ka]
    mz = send(jnp.concatenate(m[0::4], 0), moved(0, 2))
    for i in range(nz // 2):
        m[4 * i + 2] = mz[i * kb : (i + 1) * kb]
    bk = send(jnp.concatenate(b[0::2], 0), moved(1, 0))
    for d in range(0, nr, 2):
        b[d + 1] = bk[d // 2 * kb : (d // 2 + 1) * kb]
    px = half_of(a[0::2], y)
    px = sum(send(px, moved(d, 0, home)) for d in range(2, nr, 2))
    pxy = after(half_of(a[0::2], 1 - y), *a[2::2])
    pxy = sum(send(pxy, moved(d, 1, home)) for d in range(2, nr, 2))
    my = send(jnp.concatenate(m[0::2], 0), moved(0, 1))
    for d in range(nz):
        m[2 * d + 1] = my[d * kb : (d + 1) * kb]
    acx = jnp.where(row == z, half_of(a[0::2] + a[1::2], y), jnp.concatenate([px, pxy], axis=0))
    ack = send(acx, moved(1, 0, core))

    smem = pl.BlockSpec(memory_space=pltpu.SMEM)
    vmem = pl.BlockSpec(memory_space=pltpu.VMEM)
    limit = pltpu.CompilerParams(vmem_limit_bytes=40 * 1024 * 1024)
    tile = jax.ShapeDtypeStruct((tall, narrow), jnp.float32)
    part, mask = pl.pallas_call(
        functools.partial(direct, sizes),
        out_shape=(tile, tile),
        in_specs=[smem, smem] + [vmem] * (nc + nr),
        out_specs=(vmem, vmem),
        scratch_shapes=[pltpu.VMEM((ka * nc, tall), jnp.float32), pltpu.VMEM((kb * nr, narrow), jnp.float32)],
        compiler_params=limit,
    )(occ_counts, vir_counts, *a, *b)
    return pl.pallas_call(
        functools.partial(mirrored, sizes),
        out_shape=tile,
        in_specs=[vmem] * (4 + nc),
        out_specs=vmem,
        scratch_shapes=[pltpu.VMEM((kb * nr, tall), jnp.float32), pltpu.VMEM((ka * nc, narrow), jnp.float32)],
        compiler_params=limit,
    )(part, mask, *m, acx, ack)


def solution(mesh):
    nr, nc = mesh.shape["row"], mesh.shape["col"]

    def whole(amplitudes, integrals, occ_counts, vir_counts):
        pairs, kw = amplitudes.shape
        sizes = (nr, nc, pairs // nr, pairs // nc, kw // nc, kw // nr)
        placed = (P("row", "col"), P("row", "col"), P(), P())
        return jax.shard_map(
            functools.partial(per_device, sizes), mesh=mesh, in_specs=placed, out_specs=P("row", "col"), check_vma=False
        )(amplitudes, integrals, occ_counts, vir_counts)

    return whole
```

```python
import functools
import jax
import jax.numpy as jnp
from jax import lax
from jax.experimental import pallas as pl
from jax.experimental.pallas import tpu as pltpu
from jax.sharding import PartitionSpec as P

NVIR = 400
IRREPS = 8


def labels_of(pos, occ, vir):
    occ_of = pos // NVIR
    vir_of = pos - occ_of * NVIR
    one = jnp.zeros_like(pos)
    two = jnp.zeros_like(pos)
    for bound in occ:
        one = one + jnp.where(occ_of >= bound, 1, 0)
    for bound in vir:
        two = two + jnp.where(vir_of >= bound, 1, 0)
    return one ^ two


def halves(value):
    high = value.astype(jnp.bfloat16)
    return high, (value - high.astype(jnp.float32)).astype(jnp.bfloat16)


def product(left, right):
    def mm(one, two):
        return lax.dot_general(one, two, (((0,), (0,)), ((), ())), preferred_element_type=jnp.float32)

    (lh, ll), (rh, rl) = halves(left), halves(right)
    return mm(lh, rl) + mm(ll, rh) + mm(lh, rh)


def direct(sizes, *refs):
    nr, nc, tall, narrow, ka, kb = sizes
    occ_ref, vir_ref = refs[:2]
    a_refs, b_refs = refs[2 : 2 + nc], refs[2 + nc : 2 + nc + nr]
    out_ref, mask_ref, left, right = refs[2 + nc + nr :]
    row, col = lax.axis_index("row"), lax.axis_index("col")
    for d in range(nc):
        left[pl.ds(pl.multiple_of((col ^ d) * ka, ka), ka), :] = a_refs[d][...]
    for d in range(nr):
        right[pl.ds(pl.multiple_of((row ^ d) * kb, kb), kb), :] = b_refs[d][...]
    out_ref[...] = product(left[...], right[...])
    occ, vir = [], []
    one = two = 0
    for h in range(IRREPS - 1):
        one, two = one + occ_ref[h], two + vir_ref[h]
        occ.append(one)
        vir.append(two)
    rows = labels_of(row * tall + lax.broadcasted_iota(jnp.int32, (tall, 1), 0), occ, vir)
    cols = labels_of(col * narrow + lax.broadcasted_iota(jnp.int32, (1, narrow), 1), occ, vir)
    mask_ref[...] = jnp.where(rows == cols, 1.0, 0.0)


def mirrored(sizes, *refs):
    nr, nc, tall, narrow, ka, kb = sizes
    nz = nc // 2
    part_ref, mask_ref = refs[:2]
    m_refs, ac_refs = refs[2 : 2 + nc], refs[2 + nc : 4 + nc]
    out_ref, left, right = refs[4 + nc :]
    col = lax.axis_index("col")
    z, y = col // 2, lax.rem(col, 2)
    for d in range(nc):
        at = pl.multiple_of((z ^ (d // 2)) * kb, kb)
        lane = pl.multiple_of((y ^ (d % 2)) * narrow, narrow)
        left[pl.ds(at, kb), pl.ds(lane, narrow)] = m_refs[d][...]
        at = pl.multiple_of((col ^ d) * ka, ka)
        rows = pl.ds((d % 2 * nz + d // 2) * ka, ka)
        right[pl.ds(at, ka), :] = ac_refs[0][rows, :] + ac_refs[1][rows, :]
    total = part_ref[...] + product(left[...], right[...])
    out_ref[...] = jnp.where(mask_ref[...] > 0.0, total, 0.0)


def per_device(sizes, amplitudes, integrals, occ_counts, vir_counts):
    nr, nc, tall, narrow, ka, kb = sizes
    nz = nc // 2
    row, col = lax.axis_index("row"), lax.axis_index("col")
    z, y = col // 2, lax.rem(col, 2)

    def send(value, pairs):
        return lax.ppermute(value, ("row", "col"), pairs)

    def moved(dr, dc, keep=lambda r, c: True):
        return [(r * nc + c, (r ^ dr) * nc + (c ^ dc)) for r in range(nr) for c in range(nc) if keep(r, c)]

    def mirror(e):
        return [(r * nc + c, (c // 2) * nc + 2 * (r ^ e) + c % 2) for r in range(nr) for c in range(nc)]

    def after(value, *others):
        return lax.optimization_barrier((value, *others))[0]

    def half_of(chunks, part):
        return jnp.concatenate([lax.dynamic_slice_in_dim(v, part * narrow, narrow, 1) for v in chunks], axis=0)

    def home(r, c):
        return r == c // 2

    def core(r, c):
        return r % 2 == (c // 2) % 2

    at = amplitudes.T
    a = [None] * nc
    a[0] = at
    m = [None] * nc
    b = [None] * nr
    b[0] = integrals
    b[1] = send(integrals, moved(1, 0))
    pair = jnp.concatenate([integrals, b[1]], axis=0)
    for d in range(nz - 1, 0, -1):
        a[2 * d] = send(at, moved(0, 2 * d))
    for e in range(0, nz, 2):
        got = send(pair, mirror(e))
        m[2 * e], m[2 * e + 2] = got[:kb], got[kb:]
    for d in range(2, nr, 2):
        got = send(after(pair, *a[2::2]), moved(d, 0))
        b[d], b[d + 1] = got[:kb], got[kb:]
    ay = send(jnp.concatenate(a[0::2], 0), moved(0, 1))
    for d in range(nz):
        a[2 * d + 1] = ay[d * ka : (d + 1) * ka]
    px = half_of(a[0::2], y)
    px = sum(send(px, moved(d, 0, home)) for d in range(2, nr, 2))
    pxy = half_of(a[0::2], 1 - y)
    pxy = sum(send(pxy, moved(d, 1, home)) for d in range(2, nr, 2))
    my = send(jnp.concatenate(m[0::2], 0), moved(0, 1))
    for d in range(nz):
        m[2 * d + 1] = my[d * kb : (d + 1) * kb]
    acx = jnp.where(row == z, half_of(a[0::2] + a[1::2], y), jnp.concatenate([px, pxy], axis=0))
    ack = send(acx, moved(1, 0, core))

    smem = pl.BlockSpec(memory_space=pltpu.SMEM)
    vmem = pl.BlockSpec(memory_space=pltpu.VMEM)
    limit = pltpu.CompilerParams(vmem_limit_bytes=40 * 1024 * 1024)
    tile = jax.ShapeDtypeStruct((tall, narrow), jnp.float32)
    part, mask = pl.pallas_call(
        functools.partial(direct, sizes),
        out_shape=(tile, tile),
        in_specs=[smem, smem] + [vmem] * (nc + nr),
        out_specs=(vmem, vmem),
        scratch_shapes=[pltpu.VMEM((ka * nc, tall), jnp.float32), pltpu.VMEM((kb * nr, narrow), jnp.float32)],
        compiler_params=limit,
    )(occ_counts, vir_counts, *a, *b)
    return pl.pallas_call(
        functools.partial(mirrored, sizes),
        out_shape=tile,
        in_specs=[vmem] * (4 + nc),
        out_specs=vmem,
        scratch_shapes=[pltpu.VMEM((kb * nr, tall), jnp.float32), pltpu.VMEM((ka * nc, narrow), jnp.float32)],
        compiler_params=limit,
    )(part, mask, *m, acx, ack)


def solution(mesh):
    nr, nc = mesh.shape["row"], mesh.shape["col"]

    def whole(amplitudes, integrals, occ_counts, vir_counts):
        pairs, kw = amplitudes.shape
        sizes = (nr, nc, pairs // nr, pairs // nc, kw // nc, kw // nr)
        placed = (P("row", "col"), P("row", "col"), P(), P())
        return jax.shard_map(
            functools.partial(per_device, sizes), mesh=mesh, in_specs=placed, out_specs=P("row", "col"), check_vma=False
        )(amplitudes, integrals, occ_counts, vir_counts)

    return whole
```

```python
import functools
import jax
import jax.numpy as jnp
from jax import lax
from jax.experimental import pallas as pl
from jax.experimental.pallas import tpu as pltpu
from jax.sharding import PartitionSpec as P

NVIR = 400
IRREPS = 8


def labels_of(pos, occ, vir):
    occ_of = pos // NVIR
    vir_of = pos - occ_of * NVIR
    one = jnp.zeros_like(pos)
    two = jnp.zeros_like(pos)
    for bound in occ:
        one = one + jnp.where(occ_of >= bound, 1, 0)
    for bound in vir:
        two = two + jnp.where(vir_of >= bound, 1, 0)
    return one ^ two


def halves(value):
    high = value.astype(jnp.bfloat16)
    return high, (value - high.astype(jnp.float32)).astype(jnp.bfloat16)


def product(left, right):
    def mm(one, two):
        return lax.dot_general(one, two, (((0,), (0,)), ((), ())), preferred_element_type=jnp.float32)

    (lh, ll), (rh, rl) = halves(left), halves(right)
    return mm(lh, rl) + mm(ll, rh) + mm(lh, rh)


def twist(row, e):
    return (row ^ (row >> 1) ^ 1) & 1 if e // 2 % 2 == 2 else 0


def direct(sizes, *refs):
    nr, nc, tall, narrow, ka, kb = sizes
    a_refs, b_refs = refs[2 : 2 + nc], refs[2 + nc : 2 + nc + nr]
    out_ref, mask_ref, left, right, occ_ref, vir_ref, sems = refs[2 + nc + nr :]
    copies = [
        pltpu.make_async_copy(refs[0], occ_ref, sems.at[0]),
        pltpu.make_async_copy(refs[1], vir_ref, sems.at[1]),
    ]
    for copy in copies:
        copy.start()
    row, col = lax.axis_index("row"), lax.axis_index("col")
    for d in range(nc):
        left[pl.ds(pl.multiple_of((col ^ d) * ka, ka), ka), :] = a_refs[d][...]
    for d in range(nr):
        right[pl.ds(pl.multiple_of((row ^ d) * kb, kb), kb), :] = b_refs[d][...]
    out_ref[...] = product(left[...], right[...])
    for copy in copies:
        copy.wait()
    occ, vir = [], []
    one = two = 0
    for h in range(IRREPS - 1):
        one, two = one + occ_ref[h], two + vir_ref[h]
        occ.append(one)
        vir.append(two)
    rows = labels_of(row * tall + lax.broadcasted_iota(jnp.int32, (tall, 1), 0), occ, vir)
    cols = labels_of(col * narrow + lax.broadcasted_iota(jnp.int32, (1, narrow), 1), occ, vir)
    mask_ref[...] = jnp.where(rows == cols, 1.0, 0.0)


def mirrored(sizes, *refs):
    nr, nc, tall, narrow, ka, kb = sizes
    nz = nc // 2
    part_ref, mask_ref = refs[:2]
    m_refs, ac_refs = refs[2 : 2 + nc], refs[2 + nc : 4 + nc]
    out_ref, left, right = refs[4 + nc :]
    col = lax.axis_index("col")
    z, y = col // 2, lax.rem(col, 2)
    mine = lax.rem(lax.axis_index("row"), 2) == lax.rem(z, 2)
    for d in range(nc):
        at = pl.multiple_of((z ^ (d // 2) ^ twist(lax.axis_index("row"), d // 2)) * kb, kb)
        lane = pl.multiple_of((y ^ (d % 2)) * narrow, narrow)
        left[pl.ds(at, kb), pl.ds(lane, narrow)] = m_refs[d][...]
        at = pl.multiple_of((col ^ d) * ka, ka)
        rows = pl.ds((d % 2 * nz + d // 2) * ka, ka)
        right[pl.ds(at, ka), :] = jnp.where(mine, ac_refs[0][rows, :], ac_refs[1][rows, :])
    total = part_ref[...] + product(left[...], right[...])
    out_ref[...] = jnp.where(mask_ref[...] > 0.0, total, 0.0)


def per_device(sizes, amplitudes, integrals, occ_counts, vir_counts):
    nr, nc, tall, narrow, ka, kb = sizes
    nz = nc // 2
    row, col = lax.axis_index("row"), lax.axis_index("col")
    z, y = col // 2, lax.rem(col, 2)

    def send(value, pairs):
        return lax.ppermute(value, ("row", "col"), pairs)

    def moved(dr, dc, keep=lambda r, c: True):
        return [(r * nc + c, (r ^ dr) * nc + (c ^ dc)) for r in range(nr) for c in range(nc) if keep(r, c)]

    def mirror(e):
        return [(r * nc + c, (c // 2) * nc + 2 * (r ^ e ^ twist(c // 2, e)) + c % 2) for r in range(nr) for c in range(nc)]

    def after(value, *others):
        return lax.optimization_barrier((value, *others))[0]

    def half_of(chunks, part):
        return jnp.concatenate([lax.dynamic_slice_in_dim(v, part * narrow, narrow, 1) for v in chunks], axis=0)

    def home(r, c):
        return r == c // 2

    def core(r, c):
        return r % 2 == (c // 2) % 2

    at = amplitudes.T
    a = [None] * nc
    a[0] = at
    m = [None] * nc
    b = [None] * nr
    b[0] = integrals
    b[1] = send(integrals, moved(1, 0))
    pair = jnp.concatenate([integrals, b[1]], axis=0)
    for d in range(nz - 1, 0, -1):
        a[2 * d] = send(at, moved(0, 2 * d))
    for e in [e ^ 1 ^ (e // 2 % 2) for e in range(0, nz, 2)]:
        got = send(pair, mirror(e))
        m[2 * e], m[2 * (e ^ 1)] = got[:kb], got[kb:]
    for d in range(2, nr, 2):
        got = send(after(pair, *a[2::2]), moved(d, 0))
        b[d], b[d + 1] = got[:kb], got[kb:]
    ay = send(jnp.concatenate(a[0::2], 0), moved(0, 1))
    for d in range(nz):
        a[2 * d + 1] = ay[d * ka : (d + 1) * ka]
    px = half_of(a[0::2], y)
    px = sum(send(px, moved(d, 0, home)) for d in range(2, nr, 2))
    pxy = half_of(a[0::2], 1 - y)
    pxy = sum(send(pxy, moved(d, 1, home)) for d in range(2, nr, 2))
    my = send(jnp.concatenate(m[0::2], 0), moved(0, 1))
    for d in range(nz):
        m[2 * d + 1] = my[d * kb : (d + 1) * kb]
    acx = jnp.where(row == z, half_of(a[0::2] + a[1::2], y), jnp.concatenate([px, pxy], axis=0))
    ack = send(acx, moved(1, 0))

    hbm = pl.BlockSpec(memory_space=pl.ANY)
    vmem = pl.BlockSpec(memory_space=pltpu.VMEM)
    limit = pltpu.CompilerParams(vmem_limit_bytes=40 * 1024 * 1024)
    tile = jax.ShapeDtypeStruct((tall, narrow), jnp.float32)
    part, mask = pl.pallas_call(
        functools.partial(direct, sizes),
        out_shape=(tile, tile),
        in_specs=[hbm, hbm] + [vmem] * (nc + nr),
        out_specs=(vmem, vmem),
        scratch_shapes=[
            pltpu.VMEM((ka * nc, tall), jnp.float32),
            pltpu.VMEM((kb * nr, narrow), jnp.float32),
            pltpu.SMEM((IRREPS,), jnp.int32),
            pltpu.SMEM((IRREPS,), jnp.int32),
            pltpu.SemaphoreType.DMA((2,)),
        ],
        compiler_params=limit,
    )(occ_counts, vir_counts, *a, *b)
    return pl.pallas_call(
        functools.partial(mirrored, sizes),
        out_shape=tile,
        in_specs=[vmem] * (4 + nc),
        out_specs=vmem,
        scratch_shapes=[pltpu.VMEM((kb * nr, tall), jnp.float32), pltpu.VMEM((ka * nc, narrow), jnp.float32)],
        compiler_params=limit,
    )(part, mask, *m, acx, ack)


def solution(mesh):
    nr, nc = mesh.shape["row"], mesh.shape["col"]

    def whole(amplitudes, integrals, occ_counts, vir_counts):
        pairs, kw = amplitudes.shape
        sizes = (nr, nc, pairs // nr, pairs // nc, kw // nc, kw // nr)
        placed = (P("row", "col"), P("row", "col"), P(), P())
        return jax.shard_map(
            functools.partial(per_device, sizes), mesh=mesh, in_specs=placed, out_specs=P("row", "col"), check_vma=False
        )(amplitudes, integrals, occ_counts, vir_counts)

    return whole
```

```python
import functools
import jax
import jax.numpy as jnp
from jax import lax
from jax.experimental import pallas as pl
from jax.experimental.pallas import tpu as pltpu
from jax.sharding import PartitionSpec as P

NVIR = 400
IRREPS = 8


def labels_of(pos, occ, vir):
    occ_of = pos // NVIR
    vir_of = pos - occ_of * NVIR
    one = jnp.zeros_like(pos)
    two = jnp.zeros_like(pos)
    for bound in occ:
        one = one + jnp.where(occ_of >= bound, 1, 0)
    for bound in vir:
        two = two + jnp.where(vir_of >= bound, 1, 0)
    return one ^ two


def halves(value):
    high = value.astype(jnp.bfloat16)
    return high, (value - high.astype(jnp.float32)).astype(jnp.bfloat16)


def product(left, right):
    def mm(one, two):
        return lax.dot_general(one, two, (((0,), (0,)), ((), ())), preferred_element_type=jnp.float32)

    (lh, ll), (rh, rl) = halves(left), halves(right)
    return mm(lh, rl) + mm(ll, rh) + mm(lh, rh)


def shifts_of(nz):
    return [e ^ 1 ^ (e // 2 % 2) for e in range(0, nz, 2)]


def direct(sizes, occ_hbm, vir_hbm, a_ref, ay_ref, *refs):
    nr, nc, tall, narrow, ka, kb = sizes
    b_refs = refs[: nr // 2]
    out_ref, mask_ref, left, right, occ_ref, vir_ref, sems = refs[nr // 2 :]
    copies = [
        pltpu.make_async_copy(occ_hbm, occ_ref, sems.at[0]),
        pltpu.make_async_copy(vir_hbm, vir_ref, sems.at[1]),
    ]
    for copy in copies:
        copy.start()
    row, col = lax.axis_index("row"), lax.axis_index("col")
    for d in range(nc // 2):
        rows = pl.ds(d * ka, ka)
        left[pl.ds(pl.multiple_of((col ^ (2 * d)) * ka, ka), ka), :] = a_ref[rows, :]
        left[pl.ds(pl.multiple_of((col ^ (2 * d + 1)) * ka, ka), ka), :] = ay_ref[rows, :]
    for d in range(nr):
        at = pl.multiple_of((row ^ d) * kb, kb)
        right[pl.ds(at, kb), :] = b_refs[d // 2][d % 2 * kb : (d % 2 + 1) * kb, :]
    out_ref[...] = product(left[...], right[...])
    for copy in copies:
        copy.wait()
    occ, vir = [], []
    one = two = 0
    for h in range(IRREPS - 1):
        one, two = one + occ_ref[h], two + vir_ref[h]
        occ.append(one)
        vir.append(two)
    rows = labels_of(row * tall + lax.broadcasted_iota(jnp.int32, (tall, 1), 0), occ, vir)
    cols = labels_of(col * narrow + lax.broadcasted_iota(jnp.int32, (1, narrow), 1), occ, vir)
    mask_ref[...] = jnp.where(rows == cols, 1.0, 0.0)


def mirrored(sizes, part_ref, mask_ref, my_ref, acx_ref, ack_ref, *refs):
    nr, nc, tall, narrow, ka, kb = sizes
    nz = nc // 2
    m_refs = refs[: nz // 2]
    out_ref, left, right = refs[nz // 2 :]
    row, col = lax.axis_index("row"), lax.axis_index("col")
    z, y = col // 2, lax.rem(col, 2)
    mine = lax.rem(row, 2) == lax.rem(z, 2)
    own_lane = pl.ds(pl.multiple_of(y * narrow, narrow), narrow)
    other_lane = pl.ds(pl.multiple_of((1 - y) * narrow, narrow), narrow)
    for i, e in enumerate(shifts_of(nz)):
        for j in range(2):
            at = pl.ds(pl.multiple_of((z ^ e ^ j) * kb, kb), kb)
            left[at, own_lane] = m_refs[i][j * kb : (j + 1) * kb, :]
            left[at, other_lane] = my_ref[(2 * i + j) * kb : (2 * i + j + 1) * kb, :]
    for d in range(nc):
        at = pl.multiple_of((col ^ d) * ka, ka)
        rows = pl.ds((d % 2 * nz + d // 2) * ka, ka)
        right[pl.ds(at, ka), :] = jnp.where(mine, acx_ref[rows, :], ack_ref[rows, :])
    total = part_ref[...] + product(left[...], right[...])
    out_ref[...] = jnp.where(mask_ref[...] > 0.0, total, 0.0)


def per_device(sizes, amplitudes, integrals, occ_counts, vir_counts):
    nr, nc, tall, narrow, ka, kb = sizes
    nz = nc // 2
    row, col = lax.axis_index("row"), lax.axis_index("col")
    z, y = col // 2, lax.rem(col, 2)

    def send(value, pairs):
        return lax.ppermute(value, ("row", "col"), pairs)

    def moved(dr, dc, keep=lambda r, c: True):
        return [(r * nc + c, (r ^ dr) * nc + (c ^ dc)) for r in range(nr) for c in range(nc) if keep(r, c)]

    def mirror(e):
        return [(r * nc + c, (c // 2) * nc + 2 * (r ^ e) + c % 2) for r in range(nr) for c in range(nc)]

    def after(value, *others):
        return lax.optimization_barrier((value, *others))[0]

    def half_of(chunks, part):
        return jnp.concatenate([lax.dynamic_slice_in_dim(v, part * narrow, narrow, 1) for v in chunks], axis=0)

    def home(r, c):
        return r == c // 2

    swapped = send(integrals, moved(1, 0))
    pair = jnp.concatenate([integrals, swapped], axis=0)
    at = amplitudes.T
    az = [send(at, moved(0, 2 * d)) for d in range(nz - 1, 0, -1)]
    a = [at] + az[::-1]
    acat = jnp.concatenate(a, axis=0)
    m = [send(after(pair, swapped), mirror(e)) for e in shifts_of(nz)]
    b, px = [pair], 0.0
    both = after(jnp.concatenate([pair, half_of(a, y)], axis=0), swapped)
    for d in range(2, nr, 2):
        got = send(both, moved(d, 0))
        b.append(got[: 2 * kb])
        px = px + jnp.where((row ^ d) == z, got[2 * kb :], 0.0)
    ay = send(acat, moved(0, 1))
    pxy = half_of(a, 1 - y)
    pxy = sum(send(pxy, moved(d, 1, home)) for d in range(2, nr, 2))
    my = send(after(jnp.concatenate(m, axis=0), *m), moved(0, 1))
    own = half_of(a + [ay[d * ka : (d + 1) * ka] for d in range(nz)], y)
    acx = jnp.where(row == z, own, jnp.concatenate([px, pxy], axis=0))
    ack = send(after(acx, pxy), moved(1, 0))

    hbm = pl.BlockSpec(memory_space=pltpu.HBM)
    vmem = pl.BlockSpec(memory_space=pltpu.VMEM)
    limit = pltpu.CompilerParams(vmem_limit_bytes=40 * 1024 * 1024)
    tile = jax.ShapeDtypeStruct((tall, narrow), jnp.float32)
    part, mask = pl.pallas_call(
        functools.partial(direct, sizes),
        out_shape=(tile, tile),
        in_specs=[hbm, hbm] + [vmem] * (2 + nr // 2),
        out_specs=(vmem, vmem),
        scratch_shapes=[
            pltpu.VMEM((ka * nc, tall), jnp.float32),
            pltpu.VMEM((kb * nr, narrow), jnp.float32),
            pltpu.SMEM((IRREPS,), jnp.int32),
            pltpu.SMEM((IRREPS,), jnp.int32),
            pltpu.SemaphoreType.DMA((2,)),
        ],
        compiler_params=limit,
    )(after(occ_counts, *b[1:], *m), vir_counts, acat, ay, *b)
    return pl.pallas_call(
        functools.partial(mirrored, sizes),
        out_shape=tile,
        in_specs=[vmem] * (5 + nz // 2),
        out_specs=vmem,
        scratch_shapes=[pltpu.VMEM((kb * nr, tall), jnp.float32), pltpu.VMEM((ka * nc, narrow), jnp.float32)],
        compiler_params=limit,
    )(part, mask, my, acx, ack, *m)


def solution(mesh):
    nr, nc = mesh.shape["row"], mesh.shape["col"]

    def whole(amplitudes, integrals, occ_counts, vir_counts):
        pairs, kw = amplitudes.shape
        sizes = (nr, nc, pairs // nr, pairs // nc, kw // nc, kw // nr)
        placed = (P("row", "col"), P("row", "col"), P(), P())
        return jax.shard_map(
            functools.partial(per_device, sizes), mesh=mesh, in_specs=placed, out_specs=P("row", "col"), check_vma=False
        )(amplitudes, integrals, occ_counts, vir_counts)

    return whole
```

```python
import functools
import jax
import jax.numpy as jnp
from jax import lax
from jax.experimental import pallas as pl
from jax.experimental.pallas import tpu as pltpu
from jax.sharding import PartitionSpec as P

NVIR = 400
IRREPS = 8


def labels_of(pos, occ, vir):
    occ_of = pos // NVIR
    vir_of = pos - occ_of * NVIR
    one = jnp.zeros_like(pos)
    two = jnp.zeros_like(pos)
    for bound in occ:
        one = one + jnp.where(occ_of >= bound, 1, 0)
    for bound in vir:
        two = two + jnp.where(vir_of >= bound, 1, 0)
    return one ^ two


def halves(value):
    high = value.astype(jnp.bfloat16)
    return high, (value - high.astype(jnp.float32)).astype(jnp.bfloat16)


def product(left, right):
    def mm(one, two):
        return lax.dot_general(one, two, (((0,), (0,)), ((), ())), preferred_element_type=jnp.float32)

    (lh, ll), (rh, rl) = left, right
    return mm(lh, rl) + mm(ll, rh) + mm(lh, rh)


def shifts_of(nz):
    return [e ^ 1 ^ (e // 2 % 2) for e in range(0, nz, 2)]


def direct(sizes, occ_hbm, vir_hbm, a_ref, ay_ref, *refs):
    nr, nc, tall, narrow, ka, kb = sizes
    b_refs = refs[: nr // 2]
    out_ref, mask_ref, left, right, occ_ref, vir_ref, sems = refs[nr // 2 :]
    copies = [
        pltpu.make_async_copy(occ_hbm, occ_ref, sems.at[0]),
        pltpu.make_async_copy(vir_hbm, vir_ref, sems.at[1]),
    ]
    for copy in copies:
        copy.start()
    row, col = lax.axis_index("row"), lax.axis_index("col")
    for d in range(nc // 2):
        rows = pl.ds(d * ka, ka)
        left[pl.ds(pl.multiple_of((col ^ (2 * d)) * ka, ka), ka), :] = a_ref[rows, :]
        left[pl.ds(pl.multiple_of((col ^ (2 * d + 1)) * ka, ka), ka), :] = ay_ref[rows, :]
    for d in range(nr):
        at = pl.multiple_of((row ^ d) * kb, kb)
        right[pl.ds(at, kb), :] = b_refs[d // 2][d % 2 * kb : (d % 2 + 1) * kb, :]
    out_ref[...] = product(halves(left[...]), halves(right[...]))
    for copy in copies:
        copy.wait()
    occ, vir = [], []
    one = two = 0
    for h in range(IRREPS - 1):
        one, two = one + occ_ref[h], two + vir_ref[h]
        occ.append(one)
        vir.append(two)
    rows = labels_of(row * tall + lax.broadcasted_iota(jnp.int32, (tall, 1), 0), occ, vir)
    cols = labels_of(col * narrow + lax.broadcasted_iota(jnp.int32, (1, narrow), 1), occ, vir)
    mask_ref[...] = jnp.where(rows == cols, 1.0, 0.0)


def mirrored(sizes, part_ref, mask_ref, my_ref, acx_ref, ack_ref, *refs):
    nr, nc, tall, narrow, ka, kb = sizes
    nz = nc // 2
    m_refs = refs[: nz // 2]
    out_hbm, right, done, sems = refs[nz // 2 :]
    row, col = lax.axis_index("row"), lax.axis_index("col")
    z, y = col // 2, lax.rem(col, 2)
    mine = lax.rem(row, 2) == lax.rem(z, 2)
    chunks = [e ^ j for e in shifts_of(nz) for j in range(2)]
    for d in range(nc):
        at = pl.multiple_of((2 * chunks.index(d // 2) + (y ^ (d % 2))) * ka, ka)
        rows = pl.ds((d % 2 * nz + d // 2) * ka, ka)
        right[pl.ds(at, ka), :] = jnp.where(mine, acx_ref[rows, :], ack_ref[rows, :])
    right_halves = halves(right[...])
    stores = []
    for half, left in enumerate((jnp.concatenate([m_ref[...] for m_ref in m_refs], axis=0), my_ref[...])):
        rows = pl.ds(pl.multiple_of((y ^ half) * narrow, narrow), narrow)
        total = part_ref[rows, :] + product(halves(left), right_halves)
        done[half] = jnp.where(mask_ref[rows, :] > 0.0, total, 0.0)
        stores.append(pltpu.make_async_copy(done.at[half], out_hbm.at[rows, :], sems.at[half]))
        stores[half].start()
    for store in stores:
        store.wait()


def per_device(sizes, amplitudes, integrals, occ_counts, vir_counts):
    nr, nc, tall, narrow, ka, kb = sizes
    nz = nc // 2
    row, col = lax.axis_index("row"), lax.axis_index("col")
    z, y = col // 2, lax.rem(col, 2)

    def send(value, pairs):
        return lax.ppermute(value, ("row", "col"), pairs)

    def moved(dr, dc, keep=lambda r, c: True):
        return [(r * nc + c, (r ^ dr) * nc + (c ^ dc)) for r in range(nr) for c in range(nc) if keep(r, c)]

    def mirror(e):
        return [(r * nc + c, (c // 2) * nc + 2 * (r ^ e) + c % 2) for r in range(nr) for c in range(nc)]

    def after(value, *others):
        return lax.optimization_barrier((value, *others))[0]

    def half_of(chunks, part):
        return jnp.concatenate([lax.dynamic_slice_in_dim(v, part * narrow, narrow, 1) for v in chunks], axis=0)

    def home(r, c):
        return r == c // 2

    swapped = send(integrals, moved(1, 0))
    pair = jnp.concatenate([integrals, swapped], axis=0)
    at = amplitudes.T
    az = [send(at, moved(0, 2 * d)) for d in range(nz - 1, 0, -1)]
    a = [at] + az[::-1]
    acat = jnp.concatenate(a, axis=0)
    m = [send(pair, mirror(e)) for e in shifts_of(nz)]
    b, px = [pair], 0.0
    both = jnp.concatenate([pair, half_of(a, y)], axis=0)
    for d in range(2, nr, 2):
        got = send(both, moved(d, 0))
        b.append(got[: 2 * kb])
        px = px + jnp.where((row ^ d) == z, got[2 * kb :], 0.0)
    ay = send(acat, moved(0, 1))
    pxy = after(half_of(a, 1 - y), swapped)
    pxy = sum(send(pxy, moved(d, 1, home)) for d in range(2, nr, 2))
    my = send(after(jnp.concatenate(m, axis=0), *az), moved(0, 1))
    own = half_of(a + [ay[d * ka : (d + 1) * ka] for d in range(nz)], y)
    acx = jnp.where(row == z, own, jnp.concatenate([px, pxy], axis=0))
    ack = send(after(acx, *m), moved(1, 0))

    hbm = pl.BlockSpec(memory_space=pltpu.HBM)
    vmem = pl.BlockSpec(memory_space=pltpu.VMEM)
    limit = pltpu.CompilerParams(vmem_limit_bytes=40 * 1024 * 1024)
    tile = jax.ShapeDtypeStruct((tall, narrow), jnp.float32)
    part, mask = pl.pallas_call(
        functools.partial(direct, sizes),
        out_shape=(tile, tile),
        in_specs=[hbm, hbm] + [vmem] * (2 + nr // 2),
        out_specs=(vmem, vmem),
        scratch_shapes=[
            pltpu.VMEM((ka * nc, tall), jnp.float32),
            pltpu.VMEM((kb * nr, narrow), jnp.float32),
            pltpu.SMEM((IRREPS,), jnp.int32),
            pltpu.SMEM((IRREPS,), jnp.int32),
            pltpu.SemaphoreType.DMA((2,)),
        ],
        compiler_params=limit,
    )(occ_counts, vir_counts, acat, ay, *b)
    return pl.pallas_call(
        functools.partial(mirrored, sizes),
        out_shape=tile,
        in_specs=[vmem] * (5 + nz // 2),
        out_specs=hbm,
        scratch_shapes=[
            pltpu.VMEM((ka * nc, narrow), jnp.float32),
            pltpu.VMEM((2, narrow, narrow), jnp.float32),
            pltpu.SemaphoreType.DMA((2,)),
        ],
        compiler_params=limit,
    )(part, mask, my, acx, ack, *m)


def solution(mesh):
    nr, nc = mesh.shape["row"], mesh.shape["col"]

    def whole(amplitudes, integrals, occ_counts, vir_counts):
        pairs, kw = amplitudes.shape
        sizes = (nr, nc, pairs // nr, pairs // nc, kw // nc, kw // nr)
        placed = (P("row", "col"), P("row", "col"), P(), P())
        return jax.shard_map(
            functools.partial(per_device, sizes), mesh=mesh, in_specs=placed, out_specs=P("row", "col"), check_vma=False
        )(amplitudes, integrals, occ_counts, vir_counts)

    return whole
```

```python
import functools
import jax
import jax.numpy as jnp
from jax import lax
from jax.experimental import pallas as pl
from jax.experimental.pallas import tpu as pltpu
from jax.sharding import PartitionSpec as P

NVIR = 400
IRREPS = 8


def labels_of(pos, occ, vir):
    occ_of = pos // NVIR
    vir_of = pos - occ_of * NVIR
    one = jnp.zeros_like(pos)
    two = jnp.zeros_like(pos)
    for bound in occ:
        one = one + jnp.where(occ_of >= bound, 1, 0)
    for bound in vir:
        two = two + jnp.where(vir_of >= bound, 1, 0)
    return one ^ two


def halves(value):
    high = value.astype(jnp.bfloat16)
    return high, (value - high.astype(jnp.float32)).astype(jnp.bfloat16)


def product(left, right):
    def mm(one, two):
        return lax.dot_general(one, two, (((0,), (0,)), ((), ())), preferred_element_type=jnp.float32)

    (lh, ll), (rh, rl) = left, right
    return mm(lh, rl) + mm(ll, rh) + mm(lh, rh)


def shifts_of(nz):
    return [e ^ 1 ^ (e // 2 % 2) for e in range(0, nz, 2)]


def direct(sizes, occ_hbm, vir_hbm, a_ref, ay_ref, *refs):
    nr, nc, tall, narrow, ka, kb = sizes
    b_refs = refs[: nr // 2]
    out_ref, mask_ref, left, right, occ_ref, vir_ref, sems = refs[nr // 2 :]
    copies = [
        pltpu.make_async_copy(occ_hbm, occ_ref, sems.at[0]),
        pltpu.make_async_copy(vir_hbm, vir_ref, sems.at[1]),
    ]
    for copy in copies:
        copy.start()
    row, col = lax.axis_index("row"), lax.axis_index("col")
    for d in range(nc // 2):
        rows = pl.ds(d * ka, ka)
        left[pl.ds(pl.multiple_of((col ^ (2 * d)) * ka, ka), ka), :] = a_ref[rows, :]
        left[pl.ds(pl.multiple_of((col ^ (2 * d + 1)) * ka, ka), ka), :] = ay_ref[rows, :]
    for d in range(nr):
        at = pl.multiple_of((row ^ d) * kb, kb)
        right[pl.ds(at, kb), :] = b_refs[d // 2][d % 2 * kb : (d % 2 + 1) * kb, :]
    out_ref[...] = product(halves(left[...]), halves(right[...]))
    for copy in copies:
        copy.wait()
    occ, vir = [], []
    one = two = 0
    for h in range(IRREPS - 1):
        one, two = one + occ_ref[h], two + vir_ref[h]
        occ.append(one)
        vir.append(two)
    rows = labels_of(row * tall + lax.broadcasted_iota(jnp.int32, (tall, 1), 0), occ, vir)
    cols = labels_of(col * narrow + lax.broadcasted_iota(jnp.int32, (1, narrow), 1), occ, vir)
    mask_ref[...] = jnp.where(rows == cols, 1.0, 0.0).astype(jnp.bfloat16)


def mirrored(sizes, part_ref, mask_ref, my_ref, acx_ref, ack_ref, *refs):
    nr, nc, tall, narrow, ka, kb = sizes
    nz = nc // 2
    m_refs = refs[: nz // 2]
    out_hbm, right, done, sems = refs[nz // 2 :]
    row, col = lax.axis_index("row"), lax.axis_index("col")
    z, y = col // 2, lax.rem(col, 2)
    mine = lax.rem(row, 2) == lax.rem(z, 2)
    chunks = [e ^ j for e in shifts_of(nz) for j in range(2)]
    for d in range(nc):
        at = pl.multiple_of((2 * chunks.index(d // 2) + (y ^ (d % 2))) * ka, ka)
        rows = pl.ds((d % 2 * nz + d // 2) * ka, ka)
        right[pl.ds(at, ka), :] = jnp.where(mine, acx_ref[rows, :], ack_ref[rows, :])
    right_halves = halves(right[...])
    stores = []
    for half, left in enumerate((jnp.concatenate([m_ref[...] for m_ref in m_refs], axis=0), my_ref[...])):
        rows = pl.ds(pl.multiple_of((y ^ half) * narrow, narrow), narrow)
        total = part_ref[rows, :] + product(halves(left), right_halves)
        done[half] = jnp.where(mask_ref[rows, :].astype(jnp.float32) > 0.0, total, 0.0)
        stores.append(pltpu.make_async_copy(done.at[half], out_hbm.at[rows, :], sems.at[half]))
        stores[half].start()
    for store in stores:
        store.wait()


def per_device(sizes, amplitudes, integrals, occ_counts, vir_counts):
    nr, nc, tall, narrow, ka, kb = sizes
    nz = nc // 2
    row, col = lax.axis_index("row"), lax.axis_index("col")
    z, y = col // 2, lax.rem(col, 2)

    def send(value, pairs):
        return lax.ppermute(value, ("row", "col"), pairs)

    def moved(dr, dc, keep=lambda r, c: True):
        return [(r * nc + c, (r ^ dr) * nc + (c ^ dc)) for r in range(nr) for c in range(nc) if keep(r, c)]

    def mirror(e):
        return [(r * nc + c, (c // 2) * nc + 2 * (r ^ e) + c % 2) for r in range(nr) for c in range(nc)]

    def after(value, *others):
        return lax.optimization_barrier((value, *others))[0]

    def half_of(chunks, part):
        return jnp.concatenate([lax.dynamic_slice_in_dim(v, part * narrow, narrow, 1) for v in chunks], axis=0)

    def home(r, c):
        return r == c // 2

    swapped = send(integrals, moved(1, 0))
    pair = jnp.concatenate([integrals, swapped], axis=0)
    at = amplitudes.T
    az = [send(at, moved(0, 2 * d)) for d in range(nz - 1, 0, -1)]
    a = [at] + az[::-1]
    acat = jnp.concatenate(a, axis=0)
    m = [send(pair, mirror(e)) for e in shifts_of(nz)]
    b, px = [pair], 0.0
    both = jnp.concatenate([pair, half_of(a, y)], axis=0)
    for d in range(2, nr, 2):
        got = send(both, moved(d, 0))
        b.append(got[: 2 * kb])
        px = px + jnp.where((row ^ d) == z, got[2 * kb :], 0.0)
    ay = send(acat, moved(0, 1))
    pxy = after(half_of(a, 1 - y), swapped)
    pxy = sum(send(pxy, moved(d, 1, home)) for d in range(2, nr, 2))
    my = send(after(jnp.concatenate(m, axis=0), *az), moved(0, 1))
    own = half_of(a + [ay[d * ka : (d + 1) * ka] for d in range(nz)], y)
    acx = jnp.where(row == z, own, jnp.concatenate([px, pxy], axis=0))
    ack = send(after(acx, *m), moved(1, 0))

    hbm = pl.BlockSpec(memory_space=pltpu.HBM)
    vmem = pl.BlockSpec(memory_space=pltpu.VMEM)
    limit = pltpu.CompilerParams(vmem_limit_bytes=40 * 1024 * 1024)
    tile = jax.ShapeDtypeStruct((tall, narrow), jnp.float32)
    part, mask = pl.pallas_call(
        functools.partial(direct, sizes),
        out_shape=(tile, jax.ShapeDtypeStruct((tall, narrow), jnp.bfloat16)),
        in_specs=[hbm, hbm] + [vmem] * (2 + nr // 2),
        out_specs=(vmem, vmem),
        scratch_shapes=[
            pltpu.VMEM((ka * nc, tall), jnp.float32),
            pltpu.VMEM((kb * nr, narrow), jnp.float32),
            pltpu.SMEM((IRREPS,), jnp.int32),
            pltpu.SMEM((IRREPS,), jnp.int32),
            pltpu.SemaphoreType.DMA((2,)),
        ],
        compiler_params=limit,
    )(occ_counts, vir_counts, acat, ay, *b)
    return pl.pallas_call(
        functools.partial(mirrored, sizes),
        out_shape=tile,
        in_specs=[vmem] * (5 + nz // 2),
        out_specs=hbm,
        scratch_shapes=[
            pltpu.VMEM((ka * nc, narrow), jnp.float32),
            pltpu.VMEM((2, narrow, narrow), jnp.float32),
            pltpu.SemaphoreType.DMA((2,)),
        ],
        compiler_params=limit,
    )(part, mask, my, acx, ack, *m)


def solution(mesh):
    nr, nc = mesh.shape["row"], mesh.shape["col"]

    def whole(amplitudes, integrals, occ_counts, vir_counts):
        pairs, kw = amplitudes.shape
        sizes = (nr, nc, pairs // nr, pairs // nc, kw // nc, kw // nr)
        placed = (P("row", "col"), P("row", "col"), P(), P())
        return jax.shard_map(
            functools.partial(per_device, sizes), mesh=mesh, in_specs=placed, out_specs=P("row", "col"), check_vma=False
        )(amplitudes, integrals, occ_counts, vir_counts)

    return whole
```
